256 devices in a mesh: dev: 256 (over z, y, x, core).
Axes of the slice: x: 4, y: 4, z: 8, core: 2. Of those that a mesh axis runs over, the one named last changes fastest.
Arguments:
- features: bfloat16 [262144, 512], P('dev')
- centers: bfloat16 [4096, 512], P('dev')
- target_slot: int32 [262144], P('dev'), may hold values from 0 to 4095
- row_weight: float32 [262144], P('dev'), may hold values from 0.5 to 1.5
Outputs:
- feature_grad: float32 [262144, 512], P('dev')
- center_grad: float32 [4096, 512], P('dev')
The draws below stay inside these ranges and needn't reach their ends.
All inputs are finite; a program needn't handle non-finite values.
Results may differ from the reference program's by a relative error of at most 0.0051.
Values may be sent and summed in bfloat16 or wider, within the bound.
No kernel may reach another device: no remote copies, remote signals or barrier semaphores. Data moves between devices by JAX's collectives and lax.ppermute only.
A program may use at most 64 MiB of HBM per device.

```python
import math
import jax
import jax.numpy as jnp
from jax import lax

D = 512
TOTAL_ROWS = 262144
C_TOTAL = 4096


def slot_draw(key):
    return jax.random.randint(jax.random.fold_in(key, 101), (TOTAL_ROWS,), 0, C_TOTAL, dtype=jnp.int32)


def direction_draw(key):
    return jax.random.normal(jax.random.fold_in(key, 202), (C_TOTAL, D), jnp.float32) * D ** (-0.5)


def log_spread(key, shape, lower, upper):
    return jnp.exp(jax.random.uniform(key, shape, jnp.float32, math.log(lower), math.log(upper)))


def draw_target_slot(key, part):
    slot_ids = slot_draw(key)
    return slot_ids


def draw_centers(key, part):
    directions = direction_draw(key)
    key = jax.random.fold_in(key, 2)
    scales = log_spread(key, (C_TOTAL, 1), 0.01, 0.1)
    return (directions * scales).astype(jnp.bfloat16)


def draw_features(key, part):
    directions = direction_draw(key)
    slot_ids = slot_draw(key)
    key = jax.random.fold_in(key, 3)
    first, second, third = jax.random.split(key, 3)
    aligned = log_spread(first, (TOTAL_ROWS, 1), 0.1, 30.0)
    noise = jax.random.normal(second, (TOTAL_ROWS, D), jnp.float32) * D ** (-0.5)
    scales = log_spread(third, (TOTAL_ROWS, 1), 1.0, 10.0)
    return (scales * (aligned * directions[slot_ids] + noise)).astype(jnp.bfloat16)


def block_levels(own_key, shape, shards, least, high):
    factor_of = 1.0
    for dim, blocks in shards:
        draws = jax.random.uniform(jax.random.fold_in(jax.random.fold_in(own_key, 6), dim), (blocks,), jnp.float32, least / len(shards), high / len(shards))
        factor_of = factor_of * jnp.repeat(jnp.exp(draws), shape[dim] // blocks).reshape((-1,) + (1,) * (len(shape) - 1 - dim))
    return factor_of


def setup_inputs(seed: int = 0) -> dict:
    seeds = jax.random.split(jax.random.key(seed), 5)
    return {
        "features": draw_features(jax.random.fold_in(seeds[4], 71), 0),
        "centers": draw_centers(jax.random.fold_in(seeds[4], 71), 0),
        "target_slot": draw_target_slot(jax.random.fold_in(seeds[4], 71), 0),
        "row_weight": jnp.clip(0.5 + 1.0 * jax.random.uniform(seeds[3], (TOTAL_ROWS,), jnp.float32) ** block_levels(seeds[3], (TOTAL_ROWS,), ((0, 256),), -0.2, 0.2), 0.5, 1.5),
    }


logit_scale = 64.0
cos_margin = math.cos(0.5)
sin_margin = math.sin(0.5)
sine_offset = 1.01
norm_epsilon = 1e-06

def unit_rows(matrix):
    values = matrix.astype(jnp.float32)
    inverse = lax.rsqrt(lax.optimization_barrier(jnp.sum(values * values, axis=1, keepdims=True)) + norm_epsilon)
    return (inverse, values * inverse)

def project_back(inverse, unit, gradient):
    return inverse * (gradient - unit * lax.optimization_barrier(jnp.sum(gradient * unit, axis=1, keepdims=True)))

def shifted_exp(cosine, is_target):
    sines = jnp.sqrt(sine_offset - cosine * cosine)
    target_logit = logit_scale * (cosine * cos_margin - sines * sin_margin)
    logits = jnp.where(is_target, target_logit, logit_scale * cosine)
    return jnp.exp(logits - logit_scale)

def cosine_grad(cosine, is_target, exponent, totals, weights):
    sines = jnp.sqrt(sine_offset - cosine * cosine)
    onehot = is_target.astype(jnp.float32)
    logit_grad = weights[:, None] * (exponent / totals[:, None] - onehot)
    slopes = jnp.where(is_target, cos_margin + cosine * sin_margin / sines, 1.0)
    return (logit_scale * logit_grad * slopes).astype(jnp.bfloat16)

def reference(features, centers, target_slot, row_weight):
    inv_f, unit_f = unit_rows(features)
    normed_f = unit_f.astype(jnp.bfloat16)
    inv_c, unit_c = unit_rows(centers)
    normed_c = unit_c.astype(jnp.bfloat16)
    column_ids = jnp.arange(C_TOTAL, dtype=jnp.int32)
    block_rows = math.gcd(TOTAL_ROWS, 512)
    blocks = TOTAL_ROWS // block_rows

    def one_block(accumulated, inputs):
        rows_in, slot_in, weight_in = inputs
        cosine = jnp.dot(rows_in, normed_c.T, preferred_element_type=jnp.float32)
        is_target = column_ids[None, :] == slot_in[:, None]
        exponent = shifted_exp(cosine, is_target)
        totals = lax.optimization_barrier(jnp.sum(exponent, axis=1))
        grads = cosine_grad(cosine, is_target, exponent, totals, weight_in)
        row_sum = jnp.dot(grads, normed_c, preferred_element_type=jnp.float32)
        accumulated = accumulated + jnp.dot(grads.T, rows_in, preferred_element_type=jnp.float32)
        return (accumulated, row_sum)
    center_sum, row_sums = lax.scan(one_block, jnp.zeros((C_TOTAL, D), jnp.float32), (normed_f.reshape(blocks, block_rows, D), target_slot.reshape(blocks, block_rows), row_weight.reshape(blocks, block_rows)))
    row_sum = row_sums.reshape(TOTAL_ROWS, D)
    return (project_back(inv_f, unit_f, row_sum), project_back(inv_c, unit_c, center_sum))
```

```python
import math

import jax
import jax.numpy as jnp
from jax import lax
from jax.experimental import pallas as pl
from jax.experimental.pallas import tpu as pltpu
from jax.sharding import PartitionSpec as P

SIDE_Z, SIDE_Y, SIDE_X, CORES = 8, 4, 4, 2
DEVICES = SIDE_Z * SIDE_Y * SIDE_X * CORES
LINE = 4
TILE = 512
VMEM_LIMIT = 32 * 1024 * 1024

logit_scale = 64.0
cos_margin = math.cos(0.5)
sin_margin = math.sin(0.5)
sine_offset = 1.01
norm_epsilon = 1e-06
log2_e = math.log2(math.e)
scale2 = logit_scale * log2_e


def device_of(z, y, x, core):
    return ((z * SIDE_Y + y) * SIDE_X + x) * CORES + core


def coordinates(device):
    core = device % CORES
    x = device // CORES % SIDE_X
    y = device // (CORES * SIDE_X) % SIDE_Y
    z = device // (CORES * SIDE_X * SIDE_Y)
    return z, y, x, core


def core_pairs():
    return [(d, d ^ 1) for d in range(DEVICES)]


def line_shift(step):
    pairs = []
    for d in range(DEVICES):
        z, y, x, core = coordinates(d)
        if core == 0:
            pairs.append((d, device_of(z, y, (x + step) % LINE, core)))
        else:
            pairs.append((d, device_of(z, (y + step) % LINE, x, core)))
    return pairs


def plane_groups():
    groups = []
    for fixed in range(LINE):
        groups.append([device_of(z, u, fixed, 0) for z in range(SIDE_Z) for u in range(LINE)])
        groups.append([device_of(z, fixed, u, 1) for z in range(SIDE_Z) for u in range(LINE)])
    return groups


def call(kernel, outs, name, flops=0, moved=0):
    return pl.pallas_call(
        kernel,
        out_shape=outs,
        compiler_params=pltpu.CompilerParams(vmem_limit_bytes=VMEM_LIMIT),
        cost_estimate=pl.CostEstimate(flops=flops, bytes_accessed=moved, transcendentals=0),
        name=name,
    )


def unit_rows(matrix):
    values = matrix.astype(jnp.float32)
    inverse = lax.rsqrt(jnp.sum(values * values, axis=1, keepdims=True) + norm_epsilon)
    return inverse, values * inverse


def project_back(inverse, unit, gradient):
    return inverse * (gradient - unit * jnp.sum(gradient * unit, axis=1, keepdims=True))


def prepare_kernel(own_ref, other_ref, normed_ref, turned_ref):
    half = own_ref.shape[0]
    for part, ref in enumerate((own_ref, other_ref)):
        for low in range(0, half, 256):
            _, unit = unit_rows(ref[low : low + 256, :])
            rows = slice(part * half + low, part * half + low + 256)
            normed_ref[rows, :] = unit.astype(jnp.bfloat16)
            turned_ref[:, rows] = unit.T.astype(jnp.bfloat16)


def totals_kernel(chunk, first, *refs):
    if first:
        centers_ref, turned_ref, place_ref, out_ref = refs
    else:
        centers_ref, turned_ref, place_ref, before_ref, out_ref = refs
    count = centers_ref.shape[0]
    rows = turned_ref.shape[1]
    ids = lax.broadcasted_iota(jnp.int32, (count, TILE), 0) + chunk * count
    for low in range(0, rows, TILE):
        lanes = slice(low, low + TILE)
        cosine = jnp.dot(centers_ref[...], turned_ref[:, lanes], preferred_element_type=jnp.float32)
        is_target = ids == place_ref[:, lanes]
        exponent = jnp.where(is_target, 0.0, jnp.exp2(cosine * scale2 - scale2))
        total = jnp.sum(exponent, axis=0, keepdims=True)
        target = jnp.sum(jnp.where(is_target, cosine, 0.0), axis=0, keepdims=True)
        if not first:
            total = total + before_ref[0:1, lanes]
            target = target + before_ref[1:2, lanes]
        out_ref[0:1, lanes] = total
        out_ref[1:2, lanes] = target


def grads_kernel(chunk, centers_ref, normed_ref, turned_ref, place_ref, mine_ref, other_ref, weight_ref, grads_ref, term_ref):
    count = centers_ref.shape[0]
    rows = turned_ref.shape[1]
    half = rows // 2
    ids = lax.broadcasted_iota(jnp.int32, (count, TILE), 0) + chunk * count
    term = jnp.zeros(term_ref.shape, jnp.float32)
    for low in range(0, rows, TILE):
        lanes = slice(low, low + TILE)
        there = (low + half) % rows
        both = mine_ref[:, lanes] + other_ref[:, there : there + TILE]
        partial, target = both[0:1], both[1:2]
        weight = logit_scale * weight_ref[:, lanes]
        sines = jnp.sqrt(sine_offset - target * target)
        logit = logit_scale * (target * cos_margin - sines * sin_margin)
        at_target = jnp.exp(logit - logit_scale)
        total = partial + at_target
        slope = cos_margin + target * sin_margin / sines
        target_grad = weight * (at_target / total - 1.0) * slope
        shift = (jnp.log(weight) - jnp.log(total)) * log2_e - scale2
        cosine = jnp.dot(centers_ref[...], turned_ref[:, lanes], preferred_element_type=jnp.float32)
        grads = jnp.exp2(cosine * scale2 + shift)
        grads = jnp.where(ids == place_ref[:, lanes], target_grad, grads).astype(jnp.bfloat16)
        grads_ref[:, lanes] = grads
        term = term + jnp.dot(grads, normed_ref[lanes, :], preferred_element_type=jnp.float32)
    term_ref[...] = term.astype(term_ref.dtype)


def rows_kernel(half, *refs):
    centers_refs, grads_refs, out_ref = refs[:LINE], refs[LINE : 2 * LINE], refs[2 * LINE]
    count = out_ref.shape[1]
    turned = [ref[...].T for ref in centers_refs]
    for low in range(0, count, TILE):
        lanes = slice(half * count + low, half * count + low + TILE)
        total = jnp.zeros((out_ref.shape[0], TILE), jnp.float32)
        for center, ref in zip(turned, grads_refs):
            total = total + jnp.dot(center, ref[:, lanes], preferred_element_type=jnp.float32)
        out_ref[:, low : low + TILE] = total.astype(out_ref.dtype)


def feature_kernel(features_ref, mine_ref, other_ref, out_ref):
    for low in range(0, out_ref.shape[0], 256):
        rows = slice(low, low + 256)
        inverse, unit = unit_rows(features_ref[rows, :])
        gradient = (mine_ref[:, rows] + other_ref[:, rows].astype(jnp.float32)).T
        out_ref[rows, :] = project_back(inverse, unit, gradient)


def center_kernel(centers_ref, terms_ref, out_ref):
    inverse, unit = unit_rows(centers_ref[...])
    gradient = terms_ref[0].astype(jnp.float32)
    for peer in range(1, terms_ref.shape[0]):
        gradient = gradient + terms_ref[peer].astype(jnp.float32)
    out_ref[...] = project_back(inverse, unit, gradient)


def sum_kernel(own_ref, *refs):
    out_ref = refs[-1]
    total = own_ref[...].astype(jnp.float32)
    for ref in refs[:-1]:
        total = total + ref[...].astype(jnp.float32)
    out_ref[...] = total.astype(out_ref.dtype)


def per_device(features, centers, target_slot, row_weight):
    rows_dev, width = features.shape
    own_centers = centers.shape[0]
    rows = CORES * rows_dev
    count = own_centers * SIDE_Z * LINE
    groups = plane_groups()
    peers = len(groups[0])
    z, y, x, core = coordinates(lax.axis_index("dev"))

    _, unit_c = unit_rows(centers)
    normed_c = unit_c.astype(jnp.bfloat16)
    own_chunk = lax.all_to_all(
        jnp.broadcast_to(normed_c[None], (peers, own_centers, width)),
        "dev", 0, 0, axis_index_groups=groups, tiled=True,
    ).reshape(count, width)
    chunks = [own_chunk] + [lax.ppermute(own_chunk, "dev", line_shift(k)) for k in range(1, LINE)]

    features_other = lax.ppermute(features, "dev", core_pairs())
    slot_other = lax.ppermute(target_slot, "dev", core_pairs())
    weight_other = lax.ppermute(row_weight, "dev", core_pairs())
    weight = jnp.concatenate([row_weight, weight_other]).reshape(1, rows)
    slot = jnp.concatenate([target_slot, slot_other])
    slot_z, slot_y, slot_x, slot_core = coordinates(slot // own_centers)
    across = jnp.where(core == 0, slot_y, slot_x)
    along = jnp.where(core == 0, x - slot_x, y - slot_y) % LINE
    place = along * count + (slot_z * LINE + across) * own_centers + slot % own_centers
    place = jnp.where(slot_core == core, place, -1).reshape(1, rows)

    normed_f, turned_f = call(
        prepare_kernel,
        (jax.ShapeDtypeStruct((rows, width), jnp.bfloat16), jax.ShapeDtypeStruct((width, rows), jnp.bfloat16)),
        "prepare", 0, 6 * rows * width,
    )(features, features_other)

    work = 2 * count * rows * width
    mine = None
    for chunk in (0, 1, 3, 2):
        before = () if mine is None else (mine,)
        mine = call(
            lambda *refs, chunk=chunk, first=mine is None: totals_kernel(chunk, first, *refs),
            jax.ShapeDtypeStruct((2, rows), jnp.float32), "totals%d" % chunk, work, 0,
        )(chunks[chunk], turned_f, place, *before)
    other = lax.ppermute(mine, "dev", core_pairs())

    grads, terms = [None] * LINE, [None] * LINE
    for chunk in (2, 1, 3, 0):
        grads[chunk], terms[chunk] = call(
            lambda *refs, chunk=chunk: grads_kernel(chunk, *refs),
            (jax.ShapeDtypeStruct((count, rows), jnp.bfloat16), jax.ShapeDtypeStruct((count, width), jnp.bfloat16)),
            "grads%d" % chunk, 2 * work, 0,
        )(chunks[chunk], normed_f, turned_f, place, mine, other, weight)
        if chunk:
            terms[chunk] = lax.ppermute(terms[chunk], "dev", line_shift(-chunk))

    row_other = call(
        lambda *refs: rows_kernel(1, *refs), jax.ShapeDtypeStruct((width, rows_dev), jnp.bfloat16), "rows_other", 2 * work, 0,
    )(*chunks, *grads)
    row_other = lax.ppermute(row_other, "dev", core_pairs())
    row_mine = call(
        lambda *refs: rows_kernel(0, *refs), jax.ShapeDtypeStruct((width, rows_dev), jnp.float32), "rows_mine", 2 * work, 0,
    )(*chunks, *grads)
    feature_grad = call(
        feature_kernel, jax.ShapeDtypeStruct((rows_dev, width), jnp.float32), "feature_grad", 0, 8 * rows_dev * width,
    )(features, row_mine, row_other)

    line_sum = call(sum_kernel, jax.ShapeDtypeStruct((count, width), jnp.bfloat16), "line_sum", 0, 10 * count * width)(*terms)
    plane = lax.all_to_all(
        line_sum.reshape(peers, own_centers, width), "dev", 0, 0, axis_index_groups=groups, tiled=True
    )
    center_grad = call(
        center_kernel, jax.ShapeDtypeStruct((own_centers, width), jnp.float32), "center_grad", 0, 2 * count * width,
    )(centers, plane)
    return feature_grad, center_grad


def solution(mesh):
    return jax.shard_map(
        per_device,
        mesh=mesh,
        in_specs=(P("dev", None), P("dev", None), P("dev"), P("dev")),
        out_specs=(P("dev", None), P("dev", None)),
        check_vma=False,
    )
```

```python
import math

import jax
import jax.numpy as jnp
from jax import lax
from jax.experimental import pallas as pl
from jax.experimental.pallas import tpu as pltpu
from jax.sharding import PartitionSpec as P

SIDE_Z, SIDE_Y, SIDE_X, CORES = 8, 4, 4, 2
DEVICES = SIDE_Z * SIDE_Y * SIDE_X * CORES
LINE = 4
TILE = 512
PART = 256
VMEM_LIMIT = 16 * 1024 * 1024

logit_scale = 64.0
cos_margin = math.cos(0.5)
sin_margin = math.sin(0.5)
sine_offset = 1.01
norm_epsilon = 1e-06
log2_e = math.log2(math.e)
scale2 = logit_scale * log2_e


def device_of(z, y, x, core):
    return ((z * SIDE_Y + y) * SIDE_X + x) * CORES + core


def coordinates(device):
    core = device % CORES
    x = device // CORES % SIDE_X
    y = device // (CORES * SIDE_X) % SIDE_Y
    z = device // (CORES * SIDE_X * SIDE_Y)
    return z, y, x, core


def core_pairs():
    return [(d, d ^ 1) for d in range(DEVICES)]


def line_shift(step):
    pairs = []
    for d in range(DEVICES):
        z, y, x, core = coordinates(d)
        if core == 0:
            pairs.append((d, device_of(z, y, (x + step) % LINE, core)))
        else:
            pairs.append((d, device_of(z, (y + step) % LINE, x, core)))
    return pairs


def plane_groups():
    groups = []
    for fixed in range(LINE):
        groups.append([device_of(z, u, fixed, 0) for z in range(SIDE_Z) for u in range(LINE)])
        groups.append([device_of(z, fixed, u, 1) for z in range(SIDE_Z) for u in range(LINE)])
    return groups


def call(kernel, outs, name, flops=0, moved=0, in_specs=None):
    return pl.pallas_call(
        kernel,
        out_shape=outs,
        **({} if in_specs is None else {"in_specs": in_specs}),
        compiler_params=pltpu.CompilerParams(vmem_limit_bytes=VMEM_LIMIT),
        cost_estimate=pl.CostEstimate(flops=flops, bytes_accessed=moved, transcendentals=0),
        name=name,
    )


def unit_rows(matrix):
    values = matrix.astype(jnp.float32)
    inverse = lax.rsqrt(jnp.sum(values * values, axis=1, keepdims=True) + norm_epsilon)
    return inverse, values * inverse


def project_back(inverse, unit, gradient):
    return inverse * (gradient - unit * jnp.sum(gradient * unit, axis=1, keepdims=True))


def prepare_kernel(own_ref, other_ref, normed_ref, turned_ref):
    half = own_ref.shape[0]
    for part, ref in enumerate((own_ref, other_ref)):
        for low in range(0, half, 256):
            _, unit = unit_rows(ref[low : low + 256, :])
            rows = slice(part * half + low, part * half + low + 256)
            normed_ref[rows, :] = unit.astype(jnp.bfloat16)
            turned_ref[:, rows] = unit.T.astype(jnp.bfloat16)


def totals_kernel(chunk, first, *refs):
    if first:
        centers_ref, turned_ref, place_ref, out_ref, normed_ref, logits_ref = refs
    else:
        centers_ref, turned_ref, place_ref, before_ref, out_ref, normed_ref, logits_ref = refs
    count = centers_ref.shape[0]
    rows = turned_ref.shape[1]
    total = jnp.zeros((1, rows), jnp.float32) if first else before_ref[0:1, :]
    target = jnp.zeros((1, rows), jnp.float32) if first else before_ref[1:2, :]
    ids = lax.broadcasted_iota(jnp.int32, (PART, rows), 0)
    for low in range(0, count, PART):
        part = slice(low, low + PART)
        _, unit = unit_rows(centers_ref[part, :])
        normed = unit.astype(jnp.bfloat16)
        normed_ref[part, :] = normed
        logits = scale2 * jnp.dot(normed, turned_ref[...], preferred_element_type=jnp.float32)
        logits_ref[part, :] = logits
        is_target = ids == place_ref[...] - (chunk * count + low)
        exponent = jnp.where(is_target, 0.0, jnp.exp2(logits - scale2))
        total = total + jnp.sum(exponent, axis=0, keepdims=True)
        target = target + jnp.sum(jnp.where(is_target, logits, 0.0), axis=0, keepdims=True)
    out_ref[0:1, :] = total
    out_ref[1:2, :] = target


def grads_kernel(chunk, logits_ref, normed_ref, place_ref, mine_ref, other_ref, weight_ref, *refs):
    grads_ref, term_ref = refs[-2:]
    count, rows = logits_ref.shape
    half = rows // 2
    both = mine_ref[...] + jnp.concatenate([other_ref[:, half:], other_ref[:, :half]], axis=1)
    partial, target = both[0:1], both[1:2] / scale2
    weight = logit_scale * weight_ref[...]
    sines = jnp.sqrt(sine_offset - target * target)
    logit = logit_scale * (target * cos_margin - sines * sin_margin)
    at_target = jnp.exp(logit - logit_scale)
    total = partial + at_target
    slope = cos_margin + target * sin_margin / sines
    target_grad = weight * (at_target / total - 1.0) * slope
    shift = (jnp.log(weight) - jnp.log(total)) * log2_e - scale2
    ids = lax.broadcasted_iota(jnp.int32, (count, TILE), 0)
    term = jnp.zeros(term_ref.shape, jnp.float32)
    for low in range(0, rows, TILE):
        lanes = slice(low, low + TILE)
        grads = jnp.exp2(logits_ref[:, lanes] + shift[:, lanes])
        is_target = ids == place_ref[:, lanes] - chunk * count
        grads = jnp.where(is_target, target_grad[:, lanes], grads).astype(jnp.bfloat16)
        grads_ref[:, lanes] = grads
        term = term + jnp.dot(grads, normed_ref[lanes, :], preferred_element_type=jnp.float32)
    term_ref[...] = term.astype(term_ref.dtype)


def rows_kernel(*refs):
    centers_refs, grads_refs, (mine_ref, other_ref) = refs[:LINE], refs[LINE : 2 * LINE], refs[2 * LINE :]
    count = mine_ref.shape[1]
    turned = [ref[...].T for ref in centers_refs]
    for half, out_ref in ((1, other_ref), (0, mine_ref)):
        for low in range(0, count, TILE):
            lanes = slice(half * count + low, half * count + low + TILE)
            total = jnp.zeros((out_ref.shape[0], TILE), jnp.float32)
            for center, ref in zip(turned, grads_refs):
                total = total + jnp.dot(center, ref[:, lanes], preferred_element_type=jnp.float32)
            out_ref[:, low : low + TILE] = total.astype(out_ref.dtype)


def feature_kernel(features_ref, mine_ref, other_ref, out_ref):
    for low in range(0, out_ref.shape[0], 256):
        rows = slice(low, low + 256)
        inverse, unit = unit_rows(features_ref[rows, :])
        gradient = (mine_ref[:, rows] + other_ref[:, rows].astype(jnp.float32)).T
        out_ref[rows, :] = project_back(inverse, unit, gradient)


def center_kernel(centers_ref, terms_ref, out_ref):
    inverse, unit = unit_rows(centers_ref[...])
    gradient = terms_ref[0].astype(jnp.float32)
    for peer in range(1, terms_ref.shape[0]):
        gradient = gradient + terms_ref[peer].astype(jnp.float32)
    out_ref[...] = project_back(inverse, unit, gradient)


def per_device(features, centers, target_slot, row_weight):
    rows_dev, width = features.shape
    own_centers = centers.shape[0]
    rows = CORES * rows_dev
    count = own_centers * SIDE_Z * LINE
    groups = plane_groups()
    peers = len(groups[0])
    z, y, x, core = coordinates(lax.axis_index("dev"))

    features_other = lax.ppermute(features, "dev", core_pairs())
    row_facts = jnp.stack([target_slot.astype(jnp.float32), row_weight])
    row_facts = jnp.concatenate([row_facts, lax.ppermute(row_facts, "dev", core_pairs())], axis=1)
    slot, weight = row_facts[0].astype(jnp.int32), row_facts[1:2]
    slot_z, slot_y, slot_x, slot_core = coordinates(slot // own_centers)
    across = jnp.where(core == 0, slot_y, slot_x)
    along = jnp.where(core == 0, x - slot_x, y - slot_y) % LINE
    place = along * count + (slot_z * LINE + across) * own_centers + slot % own_centers
    place = jnp.where(slot_core == core, place, -1).reshape(1, rows)

    own_chunk = lax.all_to_all(
        jnp.broadcast_to(centers[None], (peers, own_centers, width)),
        "dev", 0, 0, axis_index_groups=groups, tiled=True,
    ).reshape(count, width)
    normed_f, turned_f = call(
        prepare_kernel,
        (jax.ShapeDtypeStruct((rows, width), jnp.bfloat16), jax.ShapeDtypeStruct((width, rows), jnp.bfloat16)),
        "prepare", 0, 6 * rows * width,
    )(features, features_other)
    own_chunk, place, weight = lax.optimization_barrier((own_chunk, place, weight))
    chunks = [own_chunk] + [lax.ppermute(own_chunk, "dev", line_shift(k)) for k in range(1, LINE)]

    work = 2 * count * rows * width
    mine, logits = None, [None] * LINE
    for chunk in (0, 1, 3, 2):
        before = () if mine is None else (mine,)
        mine, chunks[chunk], logits[chunk] = call(
            lambda *refs, chunk=chunk, first=mine is None: totals_kernel(chunk, first, *refs),
            (
                jax.ShapeDtypeStruct((2, rows), jnp.float32),
                jax.ShapeDtypeStruct((count, width), jnp.bfloat16),
                jax.ShapeDtypeStruct((count, rows), jnp.float32),
            ),
            "totals%d" % chunk, work, 0,
        )(chunks[chunk], turned_f, place, *before)
    other = lax.ppermute(mine, "dev", core_pairs())

    grads, terms = [None] * LINE, [None] * LINE
    held = [logits[chunk] for chunk in (2, 1, 3, 0)]
    for chunk in (2, 1, 3, 0):
        grads[chunk], terms[chunk] = call(
            lambda *refs, chunk=chunk: grads_kernel(chunk, *refs),
            (jax.ShapeDtypeStruct((count, rows), jnp.bfloat16), jax.ShapeDtypeStruct((count, width), jnp.bfloat16)),
            "grads%d" % chunk, work, 0,
            [pl.BlockSpec(memory_space=pltpu.VMEM)] * 6 + [pl.BlockSpec(memory_space=pl.ANY)] * 4,
        )(logits[chunk], normed_f, place, mine, other, weight, *held)
        if chunk:
            terms[chunk], mine = lax.optimization_barrier((terms[chunk], mine))
            terms[chunk] = lax.ppermute(terms[chunk], "dev", line_shift(-chunk))

    row_mine, row_other = call(
        rows_kernel,
        (jax.ShapeDtypeStruct((width, rows_dev), jnp.float32), jax.ShapeDtypeStruct((width, rows_dev), jnp.bfloat16)),
        "rows", 4 * work, 0,
    )(*chunks, *grads)
    row_other, terms[0] = lax.optimization_barrier((row_other, terms[0]))
    row_other = lax.ppermute(row_other, "dev", core_pairs())

    line_sum = sum(term.astype(jnp.float32) for term in terms).astype(jnp.bfloat16)
    plane = lax.all_to_all(
        line_sum.reshape(peers, own_centers, width), "dev", 0, 0, axis_index_groups=groups, tiled=True
    )
    feature_grad = call(
        feature_kernel, jax.ShapeDtypeStruct((rows_dev, width), jnp.float32), "feature_grad", 0, 8 * rows_dev * width,
    )(features, row_mine, row_other)
    center_grad = call(
        center_kernel, jax.ShapeDtypeStruct((own_centers, width), jnp.float32), "center_grad", 0, 2 * count * width,
    )(centers, plane)
    return feature_grad, center_grad


def solution(mesh):
    return jax.shard_map(
        per_device,
        mesh=mesh,
        in_specs=(P("dev", None), P("dev", None), P("dev"), P("dev")),
        out_specs=(P("dev", None), P("dev", None)),
        check_vma=False,
    )
```

```python
import math

import jax
import jax.numpy as jnp
from jax import lax
from jax.experimental import pallas as pl
from jax.experimental.pallas import tpu as pltpu
from jax.sharding import PartitionSpec as P

SIDE_Z, SIDE_Y, SIDE_X, CORES = 8, 4, 4, 2
DEVICES = SIDE_Z * SIDE_Y * SIDE_X * CORES
LINE = 4
TILE = 512
PART = 256
ORDER_IN = (0, 1, 3, 2)
ORDER_OUT = (2, 1, 3, 0)
VMEM_LIMIT = 16 * 1024 * 1024

logit_scale = 64.0
cos_margin = math.cos(0.5)
sin_margin = math.sin(0.5)
sine_offset = 1.01
norm_epsilon = 1e-06
log2_e = math.log2(math.e)
scale2 = logit_scale * log2_e


def device_of(z, y, x, core):
    return ((z * SIDE_Y + y) * SIDE_X + x) * CORES + core


def coordinates(device):
    core = device % CORES
    x = device // CORES % SIDE_X
    y = device // (CORES * SIDE_X) % SIDE_Y
    z = device // (CORES * SIDE_X * SIDE_Y)
    return z, y, x, core


def core_pairs():
    return [(d, d ^ 1) for d in range(DEVICES)]


def line_shift(step):
    pairs = []
    for d in range(DEVICES):
        z, y, x, core = coordinates(d)
        if core == 0:
            pairs.append((d, device_of(z, y, (x + step) % LINE, core)))
        else:
            pairs.append((d, device_of(z, (y + step) % LINE, x, core)))
    return pairs


def plane_groups():
    groups = []
    for fixed in range(LINE):
        groups.append([device_of(z, u, fixed, 0) for z in reversed(range(SIDE_Z)) for u in range(LINE)])
        groups.append([device_of(z, fixed, u, 1) for z in reversed(range(SIDE_Z)) for u in range(LINE)])
    return groups


def call(kernel, outs, name, flops=0, moved=0, in_specs=None):
    return pl.pallas_call(
        kernel,
        out_shape=outs,
        **({} if in_specs is None else {"in_specs": in_specs}),
        compiler_params=pltpu.CompilerParams(vmem_limit_bytes=VMEM_LIMIT),
        cost_estimate=pl.CostEstimate(flops=flops, bytes_accessed=moved, transcendentals=0),
        name=name,
    )


def unit_rows(matrix):
    values = matrix.astype(jnp.float32)
    inverse = lax.rsqrt(jnp.sum(values * values, axis=1, keepdims=True) + norm_epsilon)
    return inverse, values * inverse


def project_back(inverse, unit, gradient):
    return inverse * (gradient - unit * jnp.sum(gradient * unit, axis=1, keepdims=True))


def prepare_kernel(own_ref, other_ref, normed_ref, turned_ref):
    half = own_ref.shape[0]
    for part, ref in enumerate((own_ref, other_ref)):
        for low in range(0, half, 256):
            _, unit = unit_rows(ref[low : low + 256, :])
            rows = slice(part * half + low, part * half + low + 256)
            normed_ref[rows, :] = unit.astype(jnp.bfloat16)
            turned_ref[:, rows] = unit.T.astype(jnp.bfloat16)


def totals_kernel(chunk, first, *refs):
    if first:
        centers_ref, turned_ref, place_ref, out_ref, normed_ref, logits_ref = refs
    else:
        centers_ref, turned_ref, place_ref, before_ref, out_ref, normed_ref, logits_ref = refs
    count = centers_ref.shape[0]
    rows = turned_ref.shape[1]
    total = jnp.zeros((1, rows), jnp.float32) if first else before_ref[0:1, :]
    target = jnp.zeros((1, rows), jnp.float32) if first else before_ref[1:2, :]
    ids = lax.broadcasted_iota(jnp.int32, (PART, rows), 0)
    for low in range(0, count, PART):
        part = slice(low, low + PART)
        _, unit = unit_rows(centers_ref[part, :])
        normed = unit.astype(jnp.bfloat16)
        normed_ref[part, :] = normed
        logits = scale2 * jnp.dot(normed, turned_ref[...], preferred_element_type=jnp.float32)
        logits_ref[part, :] = logits
        is_target = ids == place_ref[...] - (chunk * count + low)
        exponent = jnp.where(is_target, 0.0, jnp.exp2(logits - scale2))
        total = total + jnp.sum(exponent, axis=0, keepdims=True)
        target = target + jnp.sum(jnp.where(is_target, logits, 0.0), axis=0, keepdims=True)
    out_ref[0:1, :] = total
    out_ref[1:2, :] = target


def grads_kernel(chunk, logits_ref, normed_ref, place_ref, mine_ref, other_ref, weight_ref, *refs):
    grads_ref, term_ref = refs[-2:]
    count, rows = logits_ref.shape
    half = rows // 2
    both = mine_ref[...] + jnp.concatenate([other_ref[:, half:], other_ref[:, :half]], axis=1)
    partial, target = both[0:1], both[1:2] / scale2
    weight = logit_scale * weight_ref[...]
    sines = jnp.sqrt(sine_offset - target * target)
    logit = logit_scale * (target * cos_margin - sines * sin_margin)
    at_target = jnp.exp(logit - logit_scale)
    total = partial + at_target
    slope = cos_margin + target * sin_margin / sines
    target_grad = weight * (at_target / total - 1.0) * slope
    shift = (jnp.log(weight) - jnp.log(total)) * log2_e - scale2
    ids = lax.broadcasted_iota(jnp.int32, (count, TILE), 0)
    term = jnp.zeros(term_ref.shape, jnp.float32)
    for low in range(0, rows, TILE):
        lanes = slice(low, low + TILE)
        grads = jnp.exp2(logits_ref[:, lanes] + shift[:, lanes])
        is_target = ids == place_ref[:, lanes] - chunk * count
        grads = jnp.where(is_target, target_grad[:, lanes], grads).astype(jnp.bfloat16)
        grads_ref[:, lanes] = grads
        term = term + jnp.dot(grads, normed_ref[lanes, :], preferred_element_type=jnp.float32)
    term_ref[...] = term.astype(term_ref.dtype)


def rows_kernel(*refs):
    centers_refs, grads_refs, (mine_ref, other_ref) = refs[:LINE], refs[LINE : 2 * LINE], refs[2 * LINE :]
    count = mine_ref.shape[1]
    turned = [ref[...].T for ref in centers_refs]
    for half, out_ref in ((1, other_ref), (0, mine_ref)):
        for low in range(0, count, TILE):
            lanes = slice(half * count + low, half * count + low + TILE)
            total = jnp.zeros((out_ref.shape[0], TILE), jnp.float32)
            for center, ref in zip(turned, grads_refs):
                total = total + jnp.dot(center, ref[:, lanes], preferred_element_type=jnp.float32)
            out_ref[:, low : low + TILE] = total.astype(out_ref.dtype)


def feature_kernel(features_ref, mine_ref, other_ref, out_ref):
    for low in range(0, out_ref.shape[0], 256):
        rows = slice(low, low + 256)
        inverse, unit = unit_rows(features_ref[rows, :])
        gradient = (mine_ref[:, rows] + other_ref[:, rows].astype(jnp.float32)).T
        out_ref[rows, :] = project_back(inverse, unit, gradient)


def center_kernel(centers_ref, terms_ref, out_ref):
    inverse, unit = unit_rows(centers_ref[...])
    gradient = terms_ref[0].astype(jnp.float32)
    for peer in range(1, terms_ref.shape[0]):
        gradient = gradient + terms_ref[peer].astype(jnp.float32)
    out_ref[...] = project_back(inverse, unit, gradient)


def per_device(features, centers, target_slot, row_weight):
    rows_dev, width = features.shape
    own_centers = centers.shape[0]
    rows = CORES * rows_dev
    count = own_centers * SIDE_Z * LINE
    groups = plane_groups()
    peers = len(groups[0])
    z, y, x, core = coordinates(lax.axis_index("dev"))

    features_other = lax.ppermute(features, "dev", core_pairs())
    row_facts = jnp.stack([target_slot.astype(jnp.float32), row_weight])
    row_facts = jnp.concatenate([row_facts, lax.ppermute(row_facts, "dev", core_pairs())], axis=1)
    slot, weight = row_facts[0].astype(jnp.int32), row_facts[1:2]
    slot_z, slot_y, slot_x, slot_core = coordinates(slot // own_centers)
    across = jnp.where(core == 0, slot_y, slot_x)
    along = jnp.where(core == 0, x - slot_x, y - slot_y) % LINE
    place = along * count + ((SIDE_Z - 1 - slot_z) * LINE + across) * own_centers + slot % own_centers
    place = jnp.where(slot_core == core, place, -1).reshape(1, rows)

    own_chunk = lax.all_to_all(
        jnp.broadcast_to(centers[None], (peers, own_centers, width)),
        "dev", 0, 0, axis_index_groups=groups, tiled=True,
    ).reshape(count, width)
    normed_f, turned_f = call(
        prepare_kernel,
        (jax.ShapeDtypeStruct((rows, width), jnp.bfloat16), jax.ShapeDtypeStruct((width, rows), jnp.bfloat16)),
        "prepare", 0, 6 * rows * width,
    )(features, features_other)
    own_chunk, place, weight = lax.optimization_barrier((own_chunk, place, weight))
    chunks = [own_chunk] + [lax.ppermute(own_chunk, "dev", line_shift(k)) for k in range(1, LINE)]

    work = 2 * count * rows * width
    mine, logits = None, [None] * LINE
    for chunk in ORDER_IN:
        before = () if mine is None else (mine,)
        mine, chunks[chunk], logits[chunk] = call(
            lambda *refs, chunk=chunk, first=mine is None: totals_kernel(chunk, first, *refs),
            (
                jax.ShapeDtypeStruct((2, rows), jnp.float32),
                jax.ShapeDtypeStruct((count, width), jnp.bfloat16),
                jax.ShapeDtypeStruct((count, rows), jnp.float32),
            ),
            "totals%d" % chunk, work, 0,
        )(chunks[chunk], turned_f, place, *before)
    other = lax.ppermute(mine, "dev", core_pairs())

    grads, terms = [None] * LINE, [None] * LINE
    held = [logits[chunk] for chunk in ORDER_OUT]
    for chunk in ORDER_OUT:
        grads[chunk], terms[chunk] = call(
            lambda *refs, chunk=chunk: grads_kernel(chunk, *refs),
            (jax.ShapeDtypeStruct((count, rows), jnp.bfloat16), jax.ShapeDtypeStruct((count, width), jnp.bfloat16)),
            "grads%d" % chunk, work, 0,
            [pl.BlockSpec(memory_space=pltpu.VMEM)] * 6 + [pl.BlockSpec(memory_space=pl.ANY)] * 4,
        )(logits[chunk], normed_f, place, mine, other, weight, *held)
        if chunk:
            terms[chunk], mine = lax.optimization_barrier((terms[chunk], mine))
            terms[chunk] = lax.ppermute(terms[chunk], "dev", line_shift(-chunk))

    row_mine, row_other = call(
        rows_kernel,
        (jax.ShapeDtypeStruct((width, rows_dev), jnp.float32), jax.ShapeDtypeStruct((width, rows_dev), jnp.bfloat16)),
        "rows", 4 * work, 0,
    )(*chunks, *grads)
    row_other, terms[0] = lax.optimization_barrier((row_other, terms[0]))
    row_other = lax.ppermute(row_other, "dev", core_pairs())

    line_sum = sum(term.astype(jnp.float32) for term in terms).astype(jnp.bfloat16)
    plane = lax.all_to_all(
        line_sum.reshape(peers, own_centers, width), "dev", 0, 0, axis_index_groups=groups, tiled=True
    )
    feature_grad = call(
        feature_kernel, jax.ShapeDtypeStruct((rows_dev, width), jnp.float32), "feature_grad", 0, 8 * rows_dev * width,
    )(features, row_mine, row_other)
    center_grad = call(
        center_kernel, jax.ShapeDtypeStruct((own_centers, width), jnp.float32), "center_grad", 0, 2 * count * width,
    )(centers, plane)
    return feature_grad, center_grad


def solution(mesh):
    return jax.shard_map(
        per_device,
        mesh=mesh,
        in_specs=(P("dev", None), P("dev", None), P("dev"), P("dev")),
        out_specs=(P("dev", None), P("dev", None)),
        check_vma=False,
    )
```

```python
import math

import jax
import jax.numpy as jnp
from jax import lax
from jax.experimental import pallas as pl
from jax.experimental.pallas import tpu as pltpu
from jax.sharding import PartitionSpec as P

SIDE_Z, SIDE_Y, SIDE_X, CORES = 8, 4, 4, 2
DEVICES = SIDE_Z * SIDE_Y * SIDE_X * CORES
LINE = 4
TILE = 512
PART = 256
ORDER_IN = (0, 1, 3, 2)
ORDER_OUT = (2, 3, 1, 0)
VMEM_LIMIT = 16 * 1024 * 1024

logit_scale = 64.0
cos_margin = math.cos(0.5)
sin_margin = math.sin(0.5)
sine_offset = 1.01
norm_epsilon = 1e-06
log2_e = math.log2(math.e)
scale2 = logit_scale * log2_e


def device_of(z, y, x, core):
    return ((z * SIDE_Y + y) * SIDE_X + x) * CORES + core


def coordinates(device):
    core = device % CORES
    x = device // CORES % SIDE_X
    y = device // (CORES * SIDE_X) % SIDE_Y
    z = device // (CORES * SIDE_X * SIDE_Y)
    return z, y, x, core


def core_pairs():
    return [(d, d ^ 1) for d in range(DEVICES)]


def line_shift(step):
    pairs = []
    for d in range(DEVICES):
        z, y, x, core = coordinates(d)
        if core == 0:
            pairs.append((d, device_of(z, y, (x + step) % LINE, core)))
        else:
            pairs.append((d, device_of(z, (y + step) % LINE, x, core)))
    return pairs


def plane_groups():
    groups = []
    for fixed in range(LINE):
        groups.append([device_of(z, u, fixed, 0) for z in reversed(range(SIDE_Z)) for u in range(LINE)])
        groups.append([device_of(z, fixed, u, 1) for z in reversed(range(SIDE_Z)) for u in range(LINE)])
    return groups


def call(kernel, outs, name, flops=0, moved=0, in_specs=None):
    return pl.pallas_call(
        kernel,
        out_shape=outs,
        **({} if in_specs is None else {"in_specs": in_specs}),
        compiler_params=pltpu.CompilerParams(vmem_limit_bytes=VMEM_LIMIT),
        cost_estimate=pl.CostEstimate(flops=flops, bytes_accessed=moved, transcendentals=0),
        name=name,
    )


def unit_rows(matrix):
    values = matrix.astype(jnp.float32)
    inverse = lax.rsqrt(jnp.sum(values * values, axis=1, keepdims=True) + norm_epsilon)
    return inverse, values * inverse


def project_back(inverse, unit, gradient):
    return inverse * (gradient - unit * jnp.sum(gradient * unit, axis=1, keepdims=True))


def prepare_kernel(own_ref, other_ref, normed_ref, turned_ref):
    half = own_ref.shape[0]
    for part, ref in enumerate((own_ref, other_ref)):
        for low in range(0, half, 256):
            _, unit = unit_rows(ref[low : low + 256, :])
            rows = slice(part * half + low, part * half + low + 256)
            normed_ref[rows, :] = unit.astype(jnp.bfloat16)
            turned_ref[:, rows] = unit.T.astype(jnp.bfloat16)


def totals_kernel(chunk, first, *refs):
    if first:
        centers_ref, turned_ref, place_ref, out_ref, normed_ref, logits_ref = refs
    else:
        centers_ref, turned_ref, place_ref, before_ref, out_ref, normed_ref, logits_ref = refs
    count = centers_ref.shape[0]
    rows = turned_ref.shape[1]
    total = jnp.zeros((1, rows), jnp.float32) if first else before_ref[0:1, :]
    target = jnp.zeros((1, rows), jnp.float32) if first else before_ref[1:2, :]
    ids = lax.broadcasted_iota(jnp.int32, (PART, rows), 0)
    for low in range(0, count, PART):
        part = slice(low, low + PART)
        _, unit = unit_rows(centers_ref[part, :])
        normed = unit.astype(jnp.bfloat16)
        normed_ref[part, :] = normed
        logits = scale2 * jnp.dot(normed, turned_ref[...], preferred_element_type=jnp.float32)
        logits_ref[part, :] = logits
        is_target = ids == place_ref[...] - (chunk * count + low)
        exponent = jnp.where(is_target, 0.0, jnp.exp2(logits - scale2))
        total = total + jnp.sum(exponent, axis=0, keepdims=True)
        target = target + jnp.sum(jnp.where(is_target, logits, 0.0), axis=0, keepdims=True)
    out_ref[0:1, :] = total
    out_ref[1:2, :] = target


def grads_kernel(chunk, logits_ref, normed_ref, place_ref, mine_ref, other_ref, weight_ref, *refs):
    grads_ref, term_ref = refs[-2:]
    count, rows = logits_ref.shape
    half = rows // 2
    both = mine_ref[...] + jnp.concatenate([other_ref[:, half:], other_ref[:, :half]], axis=1)
    partial, target = both[0:1], both[1:2] / scale2
    weight = logit_scale * weight_ref[...]
    sines = jnp.sqrt(sine_offset - target * target)
    logit = logit_scale * (target * cos_margin - sines * sin_margin)
    at_target = jnp.exp(logit - logit_scale)
    total = partial + at_target
    slope = cos_margin + target * sin_margin / sines
    target_grad = weight * (at_target / total - 1.0) * slope
    shift = (jnp.log(weight) - jnp.log(total)) * log2_e - scale2
    ids = lax.broadcasted_iota(jnp.int32, (count, TILE), 0)
    term = jnp.zeros(term_ref.shape, jnp.float32)
    for low in range(0, rows, TILE):
        lanes = slice(low, low + TILE)
        grads = jnp.exp2(logits_ref[:, lanes] + shift[:, lanes])
        is_target = ids == place_ref[:, lanes] - chunk * count
        grads = jnp.where(is_target, target_grad[:, lanes], grads).astype(jnp.bfloat16)
        grads_ref[:, lanes] = grads
        term = term + jnp.dot(grads, normed_ref[lanes, :], preferred_element_type=jnp.float32)
    term_ref[...] = term.astype(term_ref.dtype)


def rows_kernel(*refs):
    centers_refs, grads_refs, (mine_ref, other_ref) = refs[:LINE], refs[LINE : 2 * LINE], refs[2 * LINE :]
    count = mine_ref.shape[1]
    turned = [ref[...].T for ref in centers_refs]
    for half, out_ref in ((1, other_ref), (0, mine_ref)):
        for low in range(0, count, TILE):
            lanes = slice(half * count + low, half * count + low + TILE)
            total = jnp.zeros((out_ref.shape[0], TILE), jnp.float32)
            for center, ref in zip(turned, grads_refs):
                total = total + jnp.dot(center, ref[:, lanes], preferred_element_type=jnp.float32)
            out_ref[:, low : low + TILE] = total.astype(out_ref.dtype)


def feature_kernel(features_ref, mine_ref, other_ref, out_ref):
    for low in range(0, out_ref.shape[0], 256):
        rows = slice(low, low + 256)
        inverse, unit = unit_rows(features_ref[rows, :])
        gradient = (mine_ref[:, rows] + other_ref[:, rows].astype(jnp.float32)).T
        out_ref[rows, :] = project_back(inverse, unit, gradient)


def center_kernel(centers_ref, terms_ref, out_ref):
    inverse, unit = unit_rows(centers_ref[...])
    gradient = terms_ref[0].astype(jnp.float32)
    for peer in range(1, terms_ref.shape[0]):
        gradient = gradient + terms_ref[peer].astype(jnp.float32)
    out_ref[...] = project_back(inverse, unit, gradient)


def per_device(features, centers, target_slot, row_weight):
    rows_dev, width = features.shape
    own_centers = centers.shape[0]
    rows = CORES * rows_dev
    count = own_centers * SIDE_Z * LINE
    groups = plane_groups()
    peers = len(groups[0])
    z, y, x, core = coordinates(lax.axis_index("dev"))

    features_other = lax.ppermute(features, "dev", core_pairs())
    row_facts = jnp.stack([target_slot.astype(jnp.float32), row_weight])
    row_facts = jnp.concatenate([row_facts, lax.ppermute(row_facts, "dev", core_pairs())], axis=1)
    slot, weight = row_facts[0].astype(jnp.int32), row_facts[1:2]
    slot_z, slot_y, slot_x, slot_core = coordinates(slot // own_centers)
    across = jnp.where(core == 0, slot_y, slot_x)
    along = jnp.where(core == 0, x - slot_x, y - slot_y) % LINE
    place = along * count + ((SIDE_Z - 1 - slot_z) * LINE + across) * own_centers + slot % own_centers
    place = jnp.where(slot_core == core, place, -1).reshape(1, rows)

    own_chunk = lax.all_to_all(
        jnp.broadcast_to(centers[None], (peers, own_centers, width)),
        "dev", 0, 0, axis_index_groups=groups, tiled=True,
    ).reshape(count, width)
    normed_f, turned_f = call(
        prepare_kernel,
        (jax.ShapeDtypeStruct((rows, width), jnp.bfloat16), jax.ShapeDtypeStruct((width, rows), jnp.bfloat16)),
        "prepare", 0, 6 * rows * width,
    )(features, features_other)
    own_chunk, place, weight = lax.optimization_barrier((own_chunk, place, weight))
    chunks = [own_chunk] + [lax.ppermute(own_chunk, "dev", line_shift(k)) for k in range(1, LINE)]

    work = 2 * count * rows * width
    mine, logits = None, [None] * LINE
    for chunk in ORDER_IN:
        before = () if mine is None else (mine,)
        mine, chunks[chunk], logits[chunk] = call(
            lambda *refs, chunk=chunk, first=mine is None: totals_kernel(chunk, first, *refs),
            (
                jax.ShapeDtypeStruct((2, rows), jnp.float32),
                jax.ShapeDtypeStruct((count, width), jnp.bfloat16),
                jax.ShapeDtypeStruct((count, rows), jnp.float32),
            ),
            "totals%d" % chunk, work, 0,
        )(chunks[chunk], turned_f, place, *before)
    other = lax.ppermute(mine, "dev", core_pairs())

    grads, terms = [None] * LINE, [None] * LINE
    held = [logits[chunk] for chunk in ORDER_OUT]
    for chunk in ORDER_OUT:
        grads[chunk], terms[chunk] = call(
            lambda *refs, chunk=chunk: grads_kernel(chunk, *refs),
            (jax.ShapeDtypeStruct((count, rows), jnp.bfloat16), jax.ShapeDtypeStruct((count, width), jnp.bfloat16)),
            "grads%d" % chunk, work, 0,
            [pl.BlockSpec(memory_space=pltpu.VMEM)] * 6 + [pl.BlockSpec(memory_space=pl.ANY)] * 4,
        )(logits[chunk], normed_f, place, mine, other, weight, *held)
        if chunk:
            terms[chunk], mine = lax.optimization_barrier((terms[chunk], mine))
            terms[chunk] = lax.ppermute(terms[chunk], "dev", line_shift(-chunk))

    row_mine, row_other = call(
        rows_kernel,
        (jax.ShapeDtypeStruct((width, rows_dev), jnp.float32), jax.ShapeDtypeStruct((width, rows_dev), jnp.bfloat16)),
        "rows", 4 * work, 0,
    )(*chunks, *grads)
    row_other, terms[0] = lax.optimization_barrier((row_other, terms[0]))
    row_other = lax.ppermute(row_other, "dev", core_pairs())

    line_sum = sum(term.astype(jnp.float32) for term in terms).astype(jnp.bfloat16)
    plane = lax.all_to_all(
        line_sum.reshape(peers, own_centers, width), "dev", 0, 0, axis_index_groups=groups, tiled=True
    )
    feature_grad = call(
        feature_kernel, jax.ShapeDtypeStruct((rows_dev, width), jnp.float32), "feature_grad", 0, 8 * rows_dev * width,
    )(features, row_mine, row_other)
    center_grad = call(
        center_kernel, jax.ShapeDtypeStruct((own_centers, width), jnp.float32), "center_grad", 0, 2 * count * width,
    )(centers, plane)
    return feature_grad, center_grad


def solution(mesh):
    return jax.shard_map(
        per_device,
        mesh=mesh,
        in_specs=(P("dev", None), P("dev", None), P("dev"), P("dev")),
        out_specs=(P("dev", None), P("dev", None)),
        check_vma=False,
    )
```
